128 devices in a mesh: pp: 8 (over x_hi, z), ep: 16 (over x_lo, y, core).
Axes of the slice: x: 4 (x_hi: 2, x_lo: 2; x = x_hi * 2 + x_lo), y: 4, z: 4, core: 2. Of those that a mesh axis runs over, the one named last changes fastest.
Arguments:
- section_input: bfloat16 [8, 2048, 7168], P('pp', 'ep'), may hold values from -6 to 6
- forward_routes: int32 [8, 2048, 1], P('pp', 'ep'), may hold values from 0 to 3; in each aligned block of 128 rows (0 to 127, 128 to 255, ..., all dimensions but the last counted through in order) at most 40 rows name the same one
- forward_weight: float32 [8, 2048], P('pp', 'ep'), may hold values from 0.2 to 1
- saved_input: bfloat16 [8, 2048, 7168], P('pp', 'ep'), may hold values from -6 to 6
- section_grad: bfloat16 [8, 2048, 7168], P('pp', 'ep'), may hold values from -6 to 6
- backward_routes: int32 [8, 2048, 1], P('pp', 'ep'), may hold values from 0 to 3; in each aligned block of 128 rows (0 to 127, 128 to 255, ..., all dimensions but the last counted through in order) at most 40 rows name the same one
- backward_weight: float32 [8, 2048], P('pp', 'ep'), may hold values from 0.2 to 1
- norm_gain: bfloat16 [8, 7168], P('pp'), may hold values from 0.099609375 to 1.8984375
- w_gate: bfloat16 [8, 16, 1792, 1024], P('pp', 'ep'), may hold values from -0.0625 to 0.0625
- w_up: bfloat16 [8, 16, 1792, 1024], P('pp', 'ep'), may hold values from -0.0625 to 0.0625
- w_down: bfloat16 [8, 16, 1024, 1792], P('pp', 'ep'), may hold values from -0.1875 to 0.1875
Outputs:
- arrived_input: bfloat16 [8, 2048, 7168], P('pp', 'ep')
- arrived_grad: bfloat16 [8, 2048, 7168], P('pp', 'ep')
The draws below stay inside these ranges and needn't reach their ends.
Inputs may be any that keep to these rules, and one draw needn't show every extreme that they name: `forward_routes`: one expert per token. In each aligned block of 128 rows (the tokens of one device) no expert is named more than 40 times, and in every draw some expert is named exactly 40 times in some block. `backward_routes`: same law as forward_routes.
All inputs are finite; a program needn't handle non-finite values.
Results may differ from the reference program's by a relative error of at most 0.0064.
Values may be sent and summed in bfloat16 or wider, within the bound.
No kernel may reach another device: no remote copies, remote signals or barrier semaphores. Data moves between devices by JAX's collectives and lax.ppermute only.
A program may use at most 192 MiB of HBM per device.

```python
import math
import jax
import jax.numpy as jnp
import numpy as np
from jax import lax

D = 7168
FF = 1024
TOK = 128
SECTIONS = 8
EXPERTS = 4
EXPERT_SHARDS = 16
TOKENS_EP = 2048
CAP = 40
N_EP = 16


def levels(key, extent, cuts, low, largest):
    loudness, own = 1.0, jax.random.fold_in(key, 6)
    for position, parts in cuts:
        draws = jnp.exp(jax.random.uniform(jax.random.fold_in(own, position), (parts,), jnp.float32, low / len(cuts), largest / len(cuts)))
        loudness = loudness * jnp.repeat(draws, extent[position] // parts).reshape([-1 if axis == position else 1 for axis in range(len(extent))])
    return loudness


def shared_out(own_key, own, number, rows, count, top, reach, lean):
    sequence = jax.random.permutation(own_key, count)
    crowded, common = portions_of(count, rows * top, reach, lean, True), portions_of(count, rows * top, reach, lean, False)
    places = jnp.arange(count)

    def named(lengths, offset_by):
        used = int((lengths > 0).sum())
        fixed = max(1, used // 4)
        moved = fixed + (places - fixed + offset_by * (used - fixed)) % max(1, count - fixed)
        return jnp.zeros((count,), jnp.int32).at[sequence[jnp.where(places < fixed, places, moved)]].set(jnp.asarray(lengths, jnp.int32))

    lengths = jnp.where(number % 4 == 0, named(crowded, number // 4), named(common, number - number // 4 - 1))
    mixed = jax.random.permutation(jax.random.fold_in(own, 3), count)
    source_of, sink = mixed[0:count // 2 * 2:2], mixed[1:count // 2 * 2:2]
    slack = jnp.minimum(lengths[source_of] - 1, reach - lengths[sink]) // 2
    slack = jnp.where((source_of == sequence[0]) | (sink == sequence[0]) | (lengths[sink] == 0), 0, jnp.maximum(slack, 0))
    moved = jax.random.randint(jax.random.fold_in(own, 4), (count // 2,), 0, 1 << 20) % (slack + 1)
    lengths = lengths.at[source_of].add(-moved).at[sink].add(moved)
    labels = jnp.searchsorted(jnp.cumsum(lengths), jnp.arange(rows * top), side="right").astype(jnp.int32)
    listing = labels.reshape(top, rows).T
    listing = listing[jax.random.permutation(jax.random.fold_in(own, 1), rows)]
    offset_by = jax.random.randint(jax.random.fold_in(own, 2), (rows, 1), 0, top)
    return jnp.take_along_axis(listing, (jnp.arange(top)[None, :] + offset_by) % top, axis=1)


def portions_of(number_of, total, limit, lean, full):
    portions = [(1 << 20) // math.isqrt(grade ** lean) + 1 for grade in range(1, number_of + 1)]
    largest = limit if full else min(limit, max(-(-total // number_of), total * portions[0] // sum(portions)))
    least = 1 if total - largest >= number_of - 1 else 0
    holding, surplus = [largest] + [least] * (number_of - 1), total - largest - least * (number_of - 1)
    while surplus > 0:
        free = [i for i in range(1, number_of) if holding[i] < largest] or [i for i in range(1, number_of) if holding[i] < limit]
        pool, remaining = sum([portions[i] for i in free]), surplus
        for i in free:
            more = min(limit - holding[i], max(1, remaining * portions[i] // pool), surplus)
            holding[i] = holding[i] + more
            surplus = surplus - more
    return np.array(holding)


def bell_draw(key, dims, deviation, reach, cuts=(), kind=jnp.bfloat16):
    drawn = deviation * jax.random.normal(key, dims, jnp.float32)
    if cuts:
        drawn = drawn * levels(key, dims, cuts, -0.22, 0.18)
    return jnp.clip(drawn, -reach, reach).astype(kind)


def setup_inputs(seed: int = 0) -> dict:
    arg_keys = jax.random.split(jax.random.key(seed), 12)
    section_input = bell_draw(arg_keys[0], (SECTIONS, TOKENS_EP, D), 1.0, 6.0, ((0, 8), (1, 16)))
    forward_routes_keys = jax.random.split(jax.random.fold_in(arg_keys[1], 1), SECTIONS * TOKENS_EP // TOK)
    forward_routes_turns = jax.random.permutation(jax.random.fold_in(arg_keys[1], 3), SECTIONS * TOKENS_EP // TOK)
    forward_routes = jax.vmap(lambda own, number: shared_out(jax.random.fold_in(arg_keys[1], 2), own, number, TOK, EXPERTS, 1, CAP, 2))(forward_routes_keys, forward_routes_turns).reshape((SECTIONS, TOKENS_EP, 1))
    forward_weight = jnp.clip(jnp.exp(math.log(1.0) - 1.609438 * jax.random.uniform(arg_keys[2], (SECTIONS, TOKENS_EP), jnp.float32) ** levels(arg_keys[2], (SECTIONS, TOKENS_EP), ((0, 8), (1, 16)), -0.2, 0.2)), 0.2, 1.0)
    saved_input = bell_draw(arg_keys[3], (SECTIONS, TOKENS_EP, D), 1.0, 6.0, ((0, 8), (1, 16)))
    section_grad = bell_draw(arg_keys[4], (SECTIONS, TOKENS_EP, D), 1.0, 6.0, ((0, 8), (1, 16)))
    backward_routes_keys = jax.random.split(jax.random.fold_in(arg_keys[5], 1), SECTIONS * TOKENS_EP // TOK)
    backward_routes_turns = jax.random.permutation(jax.random.fold_in(arg_keys[5], 3), SECTIONS * TOKENS_EP // TOK)
    backward_routes = jax.vmap(lambda own, number: shared_out(jax.random.fold_in(arg_keys[5], 2), own, number, TOK, EXPERTS, 1, CAP, 2))(backward_routes_keys, backward_routes_turns).reshape((SECTIONS, TOKENS_EP, 1))
    backward_weight = jnp.clip(jnp.exp(math.log(1.0) - 1.609438 * jax.random.uniform(arg_keys[6], (SECTIONS, TOKENS_EP), jnp.float32) ** levels(arg_keys[6], (SECTIONS, TOKENS_EP), ((0, 8), (1, 16)), -0.2, 0.2)), 0.2, 1.0)
    norm_gain = jnp.clip(1.0 + 0.18 * jax.random.normal(arg_keys[7], (SECTIONS, D), jnp.float32), 0.099609375, 1.8984375).astype(jnp.bfloat16)
    w_gate = bell_draw(arg_keys[8], (SECTIONS, EXPERT_SHARDS, D // 4, FF), D ** -0.5, 0.0625, ((0, 8), (1, 16)))
    w_up = bell_draw(arg_keys[9], (SECTIONS, EXPERT_SHARDS, D // 4, FF), D ** -0.5, 0.0625, ((0, 8), (1, 16)))
    w_down = bell_draw(arg_keys[10], (SECTIONS, EXPERT_SHARDS, FF, D // 4), FF ** -0.5, 0.1875, ((0, 8), (1, 16)))
    return dict(section_input=section_input, forward_routes=forward_routes, forward_weight=forward_weight, saved_input=saved_input, section_grad=section_grad, backward_routes=backward_routes, backward_weight=backward_weight, norm_gain=norm_gain, w_gate=w_gate, w_up=w_up, w_down=w_down)


epsilon = 1e-06

def normalize(tokens, norm_row):
    values = tokens.astype(jnp.float32)
    inv_rms = lax.rsqrt(lax.optimization_barrier(jnp.mean(values * values, axis=-1, keepdims=True)) + epsilon)
    return values * inv_rms * norm_row.astype(jnp.float32)

def slot_rows(routes):
    one_hot = (routes[:, :, None] == jnp.arange(EXPERTS, dtype=jnp.int32)[None, None, :]).astype(jnp.int32)
    before = jnp.cumsum(one_hot, axis=1) - one_hot
    places = lax.optimization_barrier(jnp.sum(before * one_hot, axis=2))
    return (jnp.arange(N_EP, dtype=jnp.int32)[:, None] * CAP + places).astype(jnp.int32)

def to_experts(token_rows, routes, places):
    buffer = jnp.zeros((EXPERTS, N_EP * CAP, token_rows.shape[-1]), token_rows.dtype)
    return buffer.at[routes, places].set(token_rows)

def contract_last(left, right):
    return lax.dot_general(left, right, (((1,), (1,)), ((), ())), preferred_element_type=jnp.float32)

def quarter_sum(expert_rows, weights):
    quarter = D // 4
    total = jnp.zeros((expert_rows.shape[0], weights.shape[2]), jnp.float32)
    for part_idx in range(4):
        piece = expert_rows[:, part_idx * quarter:(part_idx + 1) * quarter]
        total = total + jnp.dot(piece, weights[part_idx], preferred_element_type=jnp.float32).astype(jnp.bfloat16).astype(jnp.float32)
    return total

def quarter_back(grad_rows, weights):
    quarter = D // 4
    total = jnp.zeros((grad_rows.shape[0], FF), jnp.float32)
    for part_idx in range(4):
        piece = grad_rows[:, part_idx * quarter:(part_idx + 1) * quarter]
        total = total + contract_last(piece, weights[part_idx]).astype(jnp.bfloat16).astype(jnp.float32)
    return total

def expert_forward(expert_rows, gate_w, up_w, down_w):
    gate_pre = quarter_sum(expert_rows, gate_w)
    up_pre = quarter_sum(expert_rows, up_w)
    hidden = (gate_pre * jax.nn.sigmoid(gate_pre) * up_pre).astype(jnp.bfloat16)
    return jnp.concatenate([jnp.dot(hidden, down_w[part_idx], preferred_element_type=jnp.float32).astype(jnp.bfloat16) for part_idx in range(4)], axis=1)

def expert_backward(expert_rows, grad_rows, gate_w, up_w, down_w):
    gate_pre = quarter_sum(expert_rows, gate_w)
    up_pre = quarter_sum(expert_rows, up_w)
    hidden_grad = quarter_back(grad_rows, down_w)
    sigmoid_gate = jax.nn.sigmoid(gate_pre)
    gate_grad = (hidden_grad * up_pre * sigmoid_gate * (1.0 + gate_pre * (1.0 - sigmoid_gate))).astype(jnp.bfloat16)
    up_grad = (hidden_grad * gate_pre * sigmoid_gate).astype(jnp.bfloat16)
    pieces = []
    for part_idx in range(4):
        summed = contract_last(gate_grad, gate_w[part_idx]) + contract_last(up_grad, up_w[part_idx])
        pieces.append(summed.astype(jnp.bfloat16))
    return jnp.concatenate(pieces, axis=1)

def one_section(section_args):
    section_input, forward_routes, forward_weight, saved_input, section_grad, backward_routes, backward_weight, norm_gain, w_gate, w_up, w_down = section_args
    gate_all = w_gate.reshape(EXPERTS, 4, D // 4, FF)
    up_all = w_up.reshape(EXPERTS, 4, D // 4, FF)
    down_all = w_down.reshape(EXPERTS, 4, FF, D // 4)
    routes = forward_routes[:, 0].reshape(N_EP, TOK)
    places = slot_rows(routes)
    normed = normalize(section_input, norm_gain).astype(jnp.bfloat16).reshape(N_EP, TOK, D)
    buffer = to_experts(normed, routes, places)
    outputs = jnp.stack([expert_forward(buffer[expert], gate_all[expert], up_all[expert], down_all[expert]) for expert in range(EXPERTS)])
    mixed = outputs[routes, places].reshape(TOKENS_EP, D)
    forward_out = (section_input.astype(jnp.float32) + forward_weight[:, None] * mixed.astype(jnp.float32)).astype(jnp.bfloat16)
    routes_b = backward_routes[:, 0].reshape(N_EP, TOK)
    places_b = slot_rows(routes_b)
    normed_b = normalize(saved_input, norm_gain).astype(jnp.bfloat16).reshape(N_EP, TOK, D)
    scaled = (backward_weight[:, None] * section_grad.astype(jnp.float32)).astype(jnp.bfloat16).reshape(N_EP, TOK, D)
    row_buffer = to_experts(normed_b, routes_b, places_b)
    grad_buffer = to_experts(scaled, routes_b, places_b)
    grads = jnp.stack([expert_backward(row_buffer[expert], grad_buffer[expert], gate_all[expert], up_all[expert], down_all[expert]) for expert in range(EXPERTS)])
    normed_grad = grads[routes_b, places_b].reshape(TOKENS_EP, D)
    _, pullback = jax.vjp(lambda values: normalize(values, norm_gain), saved_input.astype(jnp.float32))
    backward_out = (section_grad.astype(jnp.float32) + pullback(normed_grad.astype(jnp.float32))[0]).astype(jnp.bfloat16)
    return (forward_out, backward_out)

def reference(section_input, forward_routes, forward_weight, saved_input, section_grad, backward_routes, backward_weight, norm_gain, w_gate, w_up, w_down):
    forward_out, backward_out = lax.map(one_section, (section_input, forward_routes, forward_weight, saved_input, section_grad, backward_routes, backward_weight, norm_gain, w_gate, w_up, w_down))
    return (jnp.roll(forward_out, 1, axis=0), jnp.roll(backward_out, -1, axis=0))
```

```python
import functools

import jax
import jax.numpy as jnp
from jax import lax
from jax.experimental import pallas as pl
from jax.experimental.pallas import tpu as pltpu
from jax.sharding import PartitionSpec as P

epsilon = 1e-06
VMEM_BYTES = 40 * 1024 * 1024
FORWARD_PIECES = 2


def from_partner(value, axis, bit):
    return lax.ppermute(value, axis, [(i, i ^ 1 << bit) for i in range(lax.axis_size(axis))])


def passed_along(value, axis, by):
    count = lax.axis_size(axis)
    return lax.ppermute(value, axis, [(i, (i + by) % count) for i in range(count)])


def exchange(value):
    return lax.all_to_all(value, "ep", split_axis=0, concat_axis=0, tiled=True)


def contract(left, right, left_dim, right_dim):
    return lax.dot_general(
        left, right, (((left_dim,), (right_dim,)), ((), ())), preferred_element_type=jnp.float32
    )


def selections(routes, experts, capacity):
    tok_count = routes.shape[1]
    padded = 8 * pl.cdiv(experts, 8)
    named = routes == lax.broadcasted_iota(jnp.int32, (padded, tok_count), 0)
    earlier = lax.broadcasted_iota(jnp.int32, (tok_count, tok_count), 0) < lax.broadcasted_iota(
        jnp.int32, (tok_count, tok_count), 1
    )
    places = contract(
        named.astype(jnp.float32).astype(jnp.bfloat16),
        earlier.astype(jnp.float32).astype(jnp.bfloat16),
        1,
        0,
    )
    places = jnp.where(named, places, -1.0)
    slots = lax.broadcasted_iota(jnp.int32, (capacity, tok_count), 0).astype(jnp.float32)
    return [
        (places[e : e + 1, :] == slots).astype(jnp.float32).astype(jnp.bfloat16)
        for e in range(experts)
    ]


def as_column(row):
    count = row.shape[1]
    diagonal = lax.broadcasted_iota(jnp.int32, (count, count), 0) == lax.broadcasted_iota(
        jnp.int32, (count, count), 1
    )
    return jnp.sum(jnp.where(diagonal, row, 0.0), axis=1, keepdims=True)


def inverse_rms(tokens_ref, quarter):
    width = tokens_ref.shape[1]
    total = 0.0
    for q in range(width // quarter):
        values = tokens_ref[:, q * quarter : (q + 1) * quarter].astype(jnp.float32)
        total = total + jnp.sum(values * values, axis=1, keepdims=True)
    return lax.rsqrt(total * (1.0 / width) + epsilon)


def normed_kernel(routes_ref, tokens_ref, norm_ref, out_ref):
    shard_count, capacity, quarter = out_ref.shape
    experts = shard_count // 4
    picks = selections(routes_ref[...], experts, capacity)
    inv_rms = inverse_rms(tokens_ref, quarter)
    for q in range(4):
        columns = slice(q * quarter, (q + 1) * quarter)
        values = tokens_ref[:, columns].astype(jnp.float32)
        normed = (values * inv_rms * norm_ref[:, columns].astype(jnp.float32)).astype(jnp.bfloat16)
        for e in range(experts):
            out_ref[4 * e + q] = contract(picks[e], normed, 1, 0).astype(jnp.bfloat16)


def scaled_kernel(routes_ref, weight_ref, grad_ref, out_ref):
    shard_count, capacity, quarter = out_ref.shape
    experts = shard_count // 4
    picks = selections(routes_ref[...], experts, capacity)
    weight = as_column(weight_ref[...])
    for q in range(4):
        columns = slice(q * quarter, (q + 1) * quarter)
        scaled = (weight * grad_ref[:, columns].astype(jnp.float32)).astype(jnp.bfloat16)
        for e in range(experts):
            out_ref[4 * e + q] = contract(picks[e], scaled, 1, 0).astype(jnp.bfloat16)


def placed_back(picks, returned_ref, q):
    mixed = 0.0
    for e, pick in enumerate(picks):
        mixed = mixed + contract(pick, returned_ref[4 * e + q], 0, 0)
    return mixed


def forward_end_kernel(piece, routes_ref, weight_ref, tokens_ref, returned_ref, out_ref):
    shard_count, capacity, width = returned_ref.shape
    experts = shard_count // 4
    quarter = tokens_ref.shape[1] // 4
    picks = selections(routes_ref[...], experts, capacity)
    weight = as_column(weight_ref[...])
    for q in range(4):
        begin = q * quarter + piece * width
        tokens = tokens_ref[:, begin : begin + width].astype(jnp.float32)
        mixed = placed_back(picks, returned_ref, q)
        out_ref[:, q * width : (q + 1) * width] = (tokens + weight * mixed).astype(jnp.bfloat16)


def backward_end_kernel(routes_ref, tokens_ref, grad_ref, norm_ref, returned_ref, out_ref, pulled_ref):
    shard_count, capacity, quarter = returned_ref.shape
    experts = shard_count // 4
    width = tokens_ref.shape[1]
    picks = selections(routes_ref[...], experts, capacity)
    squares = 0.0
    along = 0.0
    for q in range(4):
        columns = slice(q * quarter, (q + 1) * quarter)
        values = tokens_ref[:, columns].astype(jnp.float32)
        pulled = placed_back(picks, returned_ref, q) * norm_ref[:, columns].astype(jnp.float32)
        pulled_ref[:, columns] = pulled
        squares = squares + jnp.sum(values * values, axis=1, keepdims=True)
        along = along + jnp.sum(values * pulled, axis=1, keepdims=True)
    inv_rms = lax.rsqrt(squares * (1.0 / width) + epsilon)
    shrink = along * (1.0 / width) * inv_rms * inv_rms * inv_rms
    for q in range(4):
        columns = slice(q * quarter, (q + 1) * quarter)
        values = tokens_ref[:, columns].astype(jnp.float32)
        own = grad_ref[:, columns].astype(jnp.float32)
        out_ref[:, columns] = (own + (pulled_ref[:, columns] * inv_rms - values * shrink)).astype(
            jnp.bfloat16
        )


def local_call(kernel, shape, *arrays, scratch=(), flops=1 << 29):
    whole = pl.BlockSpec(memory_space=pltpu.VMEM)
    moved = sum(a.size * a.dtype.itemsize for a in arrays) + 2 * functools.reduce(
        lambda a, b: a * b, shape
    )
    return pl.pallas_call(
        kernel,
        out_shape=jax.ShapeDtypeStruct(shape, jnp.bfloat16),
        in_specs=[whole] * len(arrays),
        out_specs=whole,
        scratch_shapes=list(scratch),
        compiler_params=pltpu.CompilerParams(vmem_limit_bytes=VMEM_BYTES),
        cost_estimate=pl.CostEstimate(flops=flops, bytes_accessed=2 * moved, transcendentals=0),
    )(*arrays)


def halves(rows, core):
    half = rows.shape[0] // 2
    own = lax.dynamic_slice_in_dim(rows, core * half, half, 0)
    other = lax.dynamic_slice_in_dim(rows, (1 - core) * half, half, 0)
    return own, other


def summed_over_group(own_parts, other_parts):
    sent = jnp.concatenate([part.astype(jnp.bfloat16) for part in other_parts], axis=1)
    came = from_partner(sent, "ep", 0)
    paired = jnp.concatenate(own_parts, axis=1) + came.astype(jnp.float32)
    distant = from_partner(paired.astype(jnp.bfloat16), "ep", 1)
    return paired + distant.astype(jnp.float32)


def both_halves(own, core):
    other = from_partner(own, "ep", 0)
    first = jnp.where(core == 0, own, other)
    second = jnp.where(core == 0, other, own)
    return jnp.concatenate([first, second], axis=0)


def shards(
    section_input,
    forward_routes,
    forward_weight,
    saved_input,
    section_grad,
    backward_routes,
    backward_weight,
    norm_gain,
    w_gate,
    w_up,
    w_down,
):
    experts = lax.axis_size("ep") // 4
    tok_count, model_width = section_input.shape[1:]
    capacity = tok_count * 5 // (4 * experts)
    quarter = model_width // 4
    core = lax.axis_index("ep") & 1
    gate_w = w_gate[0, 0]
    up_w = w_up[0, 0]
    down_w = w_down[0, 0]
    hidden_width = gate_w.shape[1]
    shape = (4 * experts, capacity, quarter)
    fwd_tokens = section_input[0]
    fwd_routes = forward_routes.reshape(1, tok_count)
    bwd_tokens = saved_input[0]
    cotangent = section_grad[0]
    bwd_routes = backward_routes.reshape(1, tok_count)

    send_rows = local_call(normed_kernel, shape, bwd_routes, bwd_tokens, norm_gain)
    send_grads = local_call(scaled_kernel, shape, bwd_routes, backward_weight, cotangent)
    send_fwd = local_call(normed_kernel, shape, fwd_routes, fwd_tokens, norm_gain)

    got_rows = exchange(send_rows)
    send_grads, got_rows = lax.optimization_barrier((send_grads, got_rows))
    got_grads = exchange(send_grads)
    send_fwd, got_grads = lax.optimization_barrier((send_fwd, got_grads))
    got_fwd = exchange(send_fwd)

    own, other = halves(got_rows.reshape(-1, quarter), core)
    pre = summed_over_group(
        [contract(own, gate_w, 1, 0), contract(own, up_w, 1, 0)],
        [contract(other, gate_w, 1, 0), contract(other, up_w, 1, 0)],
    )
    own, other = halves(got_grads.reshape(-1, quarter), core)
    hidden_grad = summed_over_group([contract(own, down_w, 1, 1)], [contract(other, down_w, 1, 1)])
    gate_pre = pre[:, :hidden_width]
    up_pre = pre[:, hidden_width:]
    sigmoid_gate = jax.nn.sigmoid(gate_pre)
    gate_grad = (
        hidden_grad * up_pre * sigmoid_gate * (1.0 + gate_pre * (1.0 - sigmoid_gate))
    ).astype(jnp.bfloat16)
    up_grad = (hidden_grad * gate_pre * sigmoid_gate).astype(jnp.bfloat16)
    both_grads = both_halves(jnp.concatenate([gate_grad, up_grad], axis=1), core)
    bwd_result = (
        contract(both_grads[:, :hidden_width], gate_w, 1, 1)
        + contract(both_grads[:, hidden_width:], up_w, 1, 1)
    ).astype(jnp.bfloat16)
    bwd_result, got_fwd = lax.optimization_barrier((bwd_result, got_fwd))
    bwd_returned = exchange(bwd_result.reshape(shape))

    own, other = halves(got_fwd.reshape(-1, quarter), core)
    pre = summed_over_group(
        [contract(own, gate_w, 1, 0), contract(own, up_w, 1, 0)],
        [contract(other, gate_w, 1, 0), contract(other, up_w, 1, 0)],
    )
    gate_pre = pre[:, :hidden_width]
    up_pre = pre[:, hidden_width:]
    hidden = both_halves(
        (gate_pre * jax.nn.sigmoid(gate_pre) * up_pre).astype(jnp.bfloat16), core
    )
    hidden, bwd_returned = lax.optimization_barrier((hidden, bwd_returned))

    backward_out = local_call(
        backward_end_kernel,
        (tok_count, model_width),
        bwd_routes,
        bwd_tokens,
        cotangent,
        norm_gain,
        bwd_returned,
        scratch=[pltpu.VMEM((tok_count, model_width), jnp.float32)],
    )
    arrived_grad = passed_along(backward_out, "pp", -1)

    width = quarter // FORWARD_PIECES
    pieces = []
    for piece in range(FORWARD_PIECES):
        result = contract(hidden, down_w[:, piece * width : (piece + 1) * width], 1, 0).astype(
            jnp.bfloat16
        )
        returned = exchange(result.reshape(4 * experts, capacity, width))
        layer_out = local_call(
            functools.partial(forward_end_kernel, piece),
            (tok_count, 4 * width),
            fwd_routes,
            forward_weight,
            fwd_tokens,
            returned,
        )
        pieces.append(passed_along(layer_out, "pp", 1).reshape(tok_count, 4, width))
    arrived_input = jnp.concatenate(pieces, axis=2).reshape(1, tok_count, model_width)
    return (arrived_input, arrived_grad[None])


def solution(mesh):
    placed = (
        P("pp", "ep", None),
        P("pp", "ep", None),
        P("pp", "ep"),
        P("pp", "ep", None),
        P("pp", "ep", None),
        P("pp", "ep", None),
        P("pp", "ep"),
        P("pp", None),
        P("pp", "ep", None, None),
        P("pp", "ep", None, None),
        P("pp", "ep", None, None),
    )
    return jax.shard_map(
        shards,
        mesh=mesh,
        in_specs=placed,
        out_specs=(P("pp", "ep", None), P("pp", "ep", None)),
        check_vma=False,
    )
```

```python
import functools

import jax
import jax.numpy as jnp
from jax import lax
from jax.experimental import pallas as pl
from jax.experimental.pallas import tpu as pltpu
from jax.sharding import PartitionSpec as P

epsilon = 1e-06
VMEM_BYTES = 40 * 1024 * 1024


def from_partner(value, axis, bit):
    return lax.ppermute(value, axis, [(i, i ^ 1 << bit) for i in range(lax.axis_size(axis))])


def passed_along(value, axis, by):
    count = lax.axis_size(axis)
    return lax.ppermute(value, axis, [(i, (i + by) % count) for i in range(count)])


def exchange(value):
    return lax.all_to_all(value, "ep", split_axis=0, concat_axis=0, tiled=True)


def after(value, earlier):
    return lax.optimization_barrier((value, earlier))[0]


def contract(left, right, left_dim, right_dim):
    return lax.dot_general(
        left, right, (((left_dim,), (right_dim,)), ((), ())), preferred_element_type=jnp.float32
    )


def selections(routes, experts, capacity):
    tok_count = routes.shape[1]
    padded = 8 * pl.cdiv(experts, 8)
    named = routes == lax.broadcasted_iota(jnp.int32, (padded, tok_count), 0)
    earlier = lax.broadcasted_iota(jnp.int32, (tok_count, tok_count), 0) < lax.broadcasted_iota(
        jnp.int32, (tok_count, tok_count), 1
    )
    places = contract(
        named.astype(jnp.float32).astype(jnp.bfloat16),
        earlier.astype(jnp.float32).astype(jnp.bfloat16),
        1,
        0,
    )
    places = jnp.where(named, places, -1.0)
    slots = lax.broadcasted_iota(jnp.int32, (capacity, tok_count), 0).astype(jnp.float32)
    return [
        (places[e : e + 1, :] == slots).astype(jnp.float32).astype(jnp.bfloat16)
        for e in range(experts)
    ]


def as_column(row):
    count = row.shape[1]
    diagonal = lax.broadcasted_iota(jnp.int32, (count, count), 0) == lax.broadcasted_iota(
        jnp.int32, (count, count), 1
    )
    return jnp.sum(jnp.where(diagonal, row, 0.0), axis=1, keepdims=True)


def inverse_rms(tokens_ref, quarter):
    width = tokens_ref.shape[1]
    total = 0.0
    for q in range(width // quarter):
        values = tokens_ref[:, q * quarter : (q + 1) * quarter].astype(jnp.float32)
        total = total + jnp.sum(values * values, axis=1, keepdims=True)
    return lax.rsqrt(total * (1.0 / width) + epsilon)


def normed_kernel(routes_ref, tokens_ref, norm_ref, out_ref):
    shard_count, capacity, quarter = out_ref.shape
    experts = shard_count // 4
    picks = selections(routes_ref[...], experts, capacity)
    inv_rms = inverse_rms(tokens_ref, quarter)
    for q in range(4):
        columns = slice(q * quarter, (q + 1) * quarter)
        values = tokens_ref[:, columns].astype(jnp.float32)
        normed = (values * inv_rms * norm_ref[:, columns].astype(jnp.float32)).astype(jnp.bfloat16)
        for e in range(experts):
            out_ref[4 * e + q] = contract(picks[e], normed, 1, 0).astype(jnp.bfloat16)


def scaled_kernel(routes_ref, weight_ref, grad_ref, out_ref):
    shard_count, capacity, quarter = out_ref.shape
    experts = shard_count // 4
    picks = selections(routes_ref[...], experts, capacity)
    weight = as_column(weight_ref[...])
    for q in range(4):
        columns = slice(q * quarter, (q + 1) * quarter)
        scaled = (weight * grad_ref[:, columns].astype(jnp.float32)).astype(jnp.bfloat16)
        for e in range(experts):
            out_ref[4 * e + q] = contract(picks[e], scaled, 1, 0).astype(jnp.bfloat16)


def placed_back(picks, returned_ref, q):
    mixed = 0.0
    for e, pick in enumerate(picks):
        mixed = mixed + contract(pick, returned_ref[4 * e + q], 0, 0)
    return mixed


def forward_end_kernel(routes_ref, weight_ref, tokens_ref, returned_ref, out_ref):
    shard_count, capacity, quarter = returned_ref.shape
    picks = selections(routes_ref[...], shard_count // 4, capacity)
    weight = as_column(weight_ref[...])
    for q in range(4):
        columns = slice(q * quarter, (q + 1) * quarter)
        tokens = tokens_ref[:, columns].astype(jnp.float32)
        mixed = placed_back(picks, returned_ref, q)
        out_ref[:, columns] = (tokens + weight * mixed).astype(jnp.bfloat16)


def input_grad_kernel(widths, gate_grad_ref, up_grad_ref, rows_ref, gate_ref, up_ref, first_ref, second_ref, along_ref):
    step = pl.program_id(0)
    tile = gate_ref.shape[0]
    result = contract(gate_grad_ref[...], gate_ref[...], 1, 1)
    result = (result + contract(up_grad_ref[...], up_ref[...], 1, 1)).astype(jnp.bfloat16)
    along = jnp.sum(
        result.astype(jnp.float32) * rows_ref[...].astype(jnp.float32), axis=1, keepdims=True
    )

    @pl.when(step == 0)
    def _():
        along_ref[...] = jnp.zeros_like(along_ref)

    along_ref[...] += along
    for k in range(sum(widths) // tile):
        begin = k * tile
        target, offset = (first_ref, 0) if begin < widths[0] else (second_ref, widths[0])

        @pl.when(step == k)
        def _(target=target, begin=begin - offset):
            target[:, begin : begin + tile] = result

    @pl.when(step == pl.num_programs(0) - 1)
    def _():
        total = along_ref[...]
        high = total.astype(jnp.bfloat16)
        rest = (total - high.astype(jnp.float32)).astype(jnp.bfloat16)
        lane = lax.broadcasted_iota(jnp.int32, (total.shape[0], 128), 1)
        first_ref[:, widths[0] :] = jnp.where(
            lane == 0, high.astype(jnp.float32), jnp.where(lane == 1, rest.astype(jnp.float32), 0.0)
        ).astype(jnp.bfloat16)


def backward_first_kernel(routes_ref, tokens_ref, grad_ref, norm_ref, returned_ref, out_ref, factors_ref):
    shard_count, capacity, sent = returned_ref.shape
    width = sent - 128
    model_width = tokens_ref.shape[1]
    quarter = model_width // 4
    picks = selections(routes_ref[...], shard_count // 4, capacity)
    inv_rms = inverse_rms(tokens_ref, quarter)
    along = 0.0
    for q in range(4):
        for e, pick in enumerate(picks):
            along = along + contract(pick, returned_ref[4 * e + q, :, width:], 0, 0)
    along = jnp.sum(along, axis=1, keepdims=True)
    shrink = along * (1.0 / model_width) * inv_rms * inv_rms
    lane = lax.broadcasted_iota(jnp.int32, factors_ref.shape, 1)
    factors_ref[...] = jnp.where(lane == 0, inv_rms, shrink)
    for q in range(4):
        columns = slice(q * quarter, q * quarter + width)
        pulled = 0.0
        for e, pick in enumerate(picks):
            pulled = pulled + contract(pick, returned_ref[4 * e + q, :, :width], 0, 0)
        pulled = pulled * norm_ref[:, columns].astype(jnp.float32)
        values = tokens_ref[:, columns].astype(jnp.float32)
        own = grad_ref[:, columns].astype(jnp.float32)
        out_ref[:, q * width : (q + 1) * width] = (
            own + (pulled * inv_rms - values * shrink)
        ).astype(jnp.bfloat16)


def backward_second_kernel(routes_ref, tokens_ref, grad_ref, norm_ref, factors_ref, returned_ref, out_ref):
    shard_count, capacity, width = returned_ref.shape
    quarter = tokens_ref.shape[1] // 4
    picks = selections(routes_ref[...], shard_count // 4, capacity)
    inv_rms = factors_ref[:, 0:1]
    shrink = factors_ref[:, 1:2]
    for q in range(4):
        columns = slice((q + 1) * quarter - width, (q + 1) * quarter)
        pulled = placed_back(picks, returned_ref, q) * norm_ref[:, columns].astype(jnp.float32)
        values = tokens_ref[:, columns].astype(jnp.float32)
        own = grad_ref[:, columns].astype(jnp.float32)
        out_ref[:, q * width : (q + 1) * width] = (
            own + (pulled * inv_rms - values * shrink)
        ).astype(jnp.bfloat16)


def joined_kernel(first_ref, second_ref, out_ref):
    first = first_ref.shape[1] // 4
    second = second_ref.shape[1] // 4
    for q in range(4):
        begin = q * (first + second)
        out_ref[:, begin : begin + first] = first_ref[:, q * first : (q + 1) * first]
        out_ref[:, begin + first : begin + first + second] = second_ref[
            :, q * second : (q + 1) * second
        ]


def kernel_settings(flops, moved):
    return dict(
        compiler_params=pltpu.CompilerParams(vmem_limit_bytes=VMEM_BYTES),
        cost_estimate=pl.CostEstimate(flops=flops, bytes_accessed=moved, transcendentals=0),
    )


def local_call(kernel, shapes, *arrays):
    whole = pl.BlockSpec(memory_space=pltpu.VMEM)
    moved = sum(a.size * a.dtype.itemsize for a in arrays)
    return pl.pallas_call(
        kernel,
        out_shape=shapes,
        in_specs=[whole] * len(arrays),
        out_specs=jax.tree.map(lambda _: whole, shapes),
        **kernel_settings(1 << 28, 2 * moved),
    )(*arrays)


def input_grads(both_grads, rows, gate_w, up_w, widths, tile=256):
    row_count, hidden_width = both_grads.shape[0], gate_w.shape[1]
    steps = gate_w.shape[0] // tile
    sent = (widths[0] + 128, widths[1])
    return pl.pallas_call(
        functools.partial(input_grad_kernel, widths),
        out_shape=[jax.ShapeDtypeStruct((row_count, w), jnp.bfloat16) for w in sent],
        grid=(steps,),
        in_specs=[
            pl.BlockSpec((row_count, hidden_width), lambda i: (0, 0)),
            pl.BlockSpec((row_count, hidden_width), lambda i: (0, 1)),
            pl.BlockSpec((row_count, tile), lambda i: (0, i)),
            pl.BlockSpec((tile, hidden_width), lambda i: (i, 0)),
            pl.BlockSpec((tile, hidden_width), lambda i: (i, 0)),
        ],
        out_specs=[pl.BlockSpec((row_count, w), lambda i: (0, 0)) for w in sent],
        scratch_shapes=[pltpu.VMEM((row_count, 1), jnp.float32)],
        **kernel_settings(
            4 * row_count * hidden_width * gate_w.shape[0], 4 * gate_w.size + 4 * both_grads.size
        ),
    )(both_grads, both_grads, rows, gate_w, up_w)


def halves(rows, core):
    half = rows.shape[0] // 2
    own = lax.dynamic_slice_in_dim(rows, core * half, half, 0)
    other = lax.dynamic_slice_in_dim(rows, (1 - core) * half, half, 0)
    return own, other


def summed_over_group(own_parts, other_parts):
    sent = jnp.concatenate([part.astype(jnp.bfloat16) for part in other_parts], axis=1)
    came = from_partner(sent, "ep", 0)
    paired = jnp.concatenate(own_parts, axis=1) + came.astype(jnp.float32)
    distant = from_partner(paired.astype(jnp.bfloat16), "ep", 1)
    return paired + distant.astype(jnp.float32)


def both_halves(own, core):
    other = from_partner(own, "ep", 0)
    first = jnp.where(core == 0, own, other)
    second = jnp.where(core == 0, other, own)
    return jnp.concatenate([first, second], axis=0)


def shards(
    section_input,
    forward_routes,
    forward_weight,
    saved_input,
    section_grad,
    backward_routes,
    backward_weight,
    norm_gain,
    w_gate,
    w_up,
    w_down,
):
    experts = lax.axis_size("ep") // 4
    tok_count, model_width = section_input.shape[1:]
    capacity = tok_count * 5 // (4 * experts)
    quarter = model_width // 4
    core = lax.axis_index("ep") & 1
    gate_w = w_gate[0, 0]
    up_w = w_up[0, 0]
    down_w = w_down[0, 0]
    hidden_width = gate_w.shape[1]
    shape = (4 * experts, capacity, quarter)
    block = jax.ShapeDtypeStruct(shape, jnp.bfloat16)
    whole = jax.ShapeDtypeStruct((tok_count, model_width), jnp.bfloat16)
    widths = (quarter * 3 // 7, quarter * 4 // 7)
    fwd_tokens = section_input[0]
    fwd_routes = forward_routes.reshape(1, tok_count)
    bwd_tokens = saved_input[0]
    cotangent = section_grad[0]
    bwd_routes = backward_routes.reshape(1, tok_count)

    send_fwd = local_call(normed_kernel, block, fwd_routes, fwd_tokens, norm_gain)
    send_rows = local_call(normed_kernel, block, bwd_routes, bwd_tokens, norm_gain)
    send_grads = local_call(scaled_kernel, block, bwd_routes, backward_weight, cotangent)

    got_fwd = exchange(send_fwd)
    got_rows = exchange(after(send_rows, got_fwd))
    got_grads = exchange(after(send_grads, got_rows))

    own, other = halves(got_fwd.reshape(-1, quarter), core)
    pre = summed_over_group(
        [contract(own, gate_w, 1, 0), contract(own, up_w, 1, 0)],
        [contract(other, gate_w, 1, 0), contract(other, up_w, 1, 0)],
    )
    gate_pre = pre[:, :hidden_width]
    up_pre = pre[:, hidden_width:]
    hidden = both_halves(
        (gate_pre * jax.nn.sigmoid(gate_pre) * up_pre).astype(jnp.bfloat16), core
    )
    fwd_result = contract(hidden, down_w, 1, 0).astype(jnp.bfloat16).reshape(shape)
    fwd_returned = exchange(after(fwd_result, got_grads))

    rows = got_rows.reshape(-1, quarter)
    own, other = halves(rows, core)
    pre = summed_over_group(
        [contract(own, gate_w, 1, 0), contract(own, up_w, 1, 0)],
        [contract(other, gate_w, 1, 0), contract(other, up_w, 1, 0)],
    )
    own, other = halves(got_grads.reshape(-1, quarter), core)
    hidden_grad = summed_over_group([contract(own, down_w, 1, 1)], [contract(other, down_w, 1, 1)])
    gate_pre = pre[:, :hidden_width]
    up_pre = pre[:, hidden_width:]
    sigmoid_gate = jax.nn.sigmoid(gate_pre)
    gate_grad = (
        hidden_grad * up_pre * sigmoid_gate * (1.0 + gate_pre * (1.0 - sigmoid_gate))
    ).astype(jnp.bfloat16)
    up_grad = (hidden_grad * gate_pre * sigmoid_gate).astype(jnp.bfloat16)
    both_grads = both_halves(jnp.concatenate([gate_grad, up_grad], axis=1), core)
    both_grads, fwd_returned = lax.optimization_barrier((both_grads, fwd_returned))
    first, second = input_grads(both_grads, rows, gate_w, up_w, widths)
    first_back = exchange(first.reshape(4 * experts, capacity, -1))
    second_back = exchange(after(second, first_back).reshape(4 * experts, capacity, -1))

    layer_out = local_call(
        forward_end_kernel, whole, fwd_routes, forward_weight, fwd_tokens, fwd_returned
    )
    arrived_input = passed_along(layer_out, "pp", 1)

    first_out, factors = local_call(
        backward_first_kernel,
        [
            jax.ShapeDtypeStruct((tok_count, 4 * widths[0]), jnp.bfloat16),
            jax.ShapeDtypeStruct((tok_count, 128), jnp.float32),
        ],
        bwd_routes,
        bwd_tokens,
        cotangent,
        norm_gain,
        first_back,
    )
    second_out = local_call(
        backward_second_kernel,
        jax.ShapeDtypeStruct((tok_count, 4 * widths[1]), jnp.bfloat16),
        bwd_routes,
        bwd_tokens,
        cotangent,
        norm_gain,
        factors,
        second_back,
    )
    arrived_grad = local_call(
        joined_kernel,
        whole,
        passed_along(first_out, "pp", -1),
        passed_along(second_out, "pp", -1),
    )
    return (arrived_input[None], arrived_grad[None])


def solution(mesh):
    placed = (
        P("pp", "ep", None),
        P("pp", "ep", None),
        P("pp", "ep"),
        P("pp", "ep", None),
        P("pp", "ep", None),
        P("pp", "ep", None),
        P("pp", "ep"),
        P("pp", None),
        P("pp", "ep", None, None),
        P("pp", "ep", None, None),
        P("pp", "ep", None, None),
    )
    return jax.shard_map(
        shards,
        mesh=mesh,
        in_specs=placed,
        out_specs=(P("pp", "ep", None), P("pp", "ep", None)),
        check_vma=False,
    )
```

```python
import functools

import jax
import jax.numpy as jnp
from jax import lax
from jax.experimental import pallas as pl
from jax.experimental.pallas import tpu as pltpu
from jax.sharding import PartitionSpec as P

epsilon = 1e-06
VMEM_BYTES = 60 * 1024 * 1024
LOCAL_VMEM_BYTES = 36 * 1024 * 1024


def from_partner(value, axis, bit):
    return lax.ppermute(value, axis, [(i, i ^ 1 << bit) for i in range(lax.axis_size(axis))])


def passed_along(value, axis, by):
    count = lax.axis_size(axis)
    return lax.ppermute(value, axis, [(i, (i + by) % count) for i in range(count)])


def exchange(value):
    return lax.all_to_all(value, "ep", split_axis=0, concat_axis=0, tiled=True)


def after(value, earlier):
    return lax.optimization_barrier((value, earlier))[0]


def contract(left, right, left_dim, right_dim):
    return lax.dot_general(
        left, right, (((left_dim,), (right_dim,)), ((), ())), preferred_element_type=jnp.float32
    )


def selections(routes, experts, capacity):
    tok_count = routes.shape[1]
    padded = 8 * pl.cdiv(experts, 8)
    named = routes == lax.broadcasted_iota(jnp.int32, (padded, tok_count), 0)
    earlier = lax.broadcasted_iota(jnp.int32, (tok_count, tok_count), 0) < lax.broadcasted_iota(
        jnp.int32, (tok_count, tok_count), 1
    )
    places = contract(
        named.astype(jnp.float32).astype(jnp.bfloat16),
        earlier.astype(jnp.float32).astype(jnp.bfloat16),
        1,
        0,
    )
    places = jnp.where(named, places, -1.0)
    slots = lax.broadcasted_iota(jnp.int32, (capacity, tok_count), 0).astype(jnp.float32)
    return [
        (places[e : e + 1, :] == slots).astype(jnp.float32).astype(jnp.bfloat16)
        for e in range(experts)
    ]


def as_column(row):
    count = row.shape[1]
    diagonal = lax.broadcasted_iota(jnp.int32, (count, count), 0) == lax.broadcasted_iota(
        jnp.int32, (count, count), 1
    )
    return jnp.sum(jnp.where(diagonal, row, 0.0), axis=1, keepdims=True)


def inverse_rms(tokens_ref, quarter):
    width = tokens_ref.shape[1]
    total = 0.0
    for q in range(width // quarter):
        values = tokens_ref[:, q * quarter : (q + 1) * quarter].astype(jnp.float32)
        total = total + jnp.sum(values * values, axis=1, keepdims=True)
    return lax.rsqrt(total * (1.0 / width) + epsilon)


def normed_kernel(routes_ref, tokens_ref, norm_ref, out_ref, picks_ref, inv_rms_ref):
    experts, _, capacity, quarter = out_ref.shape
    q = pl.program_id(0)

    @pl.when(q == 0)
    def _():
        for e, pick in enumerate(selections(routes_ref[...], experts, capacity)):
            picks_ref[e] = pick
        inv_rms_ref[...] = inverse_rms(tokens_ref, quarter)

    columns = pl.ds(pl.multiple_of(q * quarter, 128), quarter)
    values = tokens_ref[:, columns].astype(jnp.float32)
    norm = norm_ref[:, columns].astype(jnp.float32)
    normed = (values * inv_rms_ref[...] * norm).astype(jnp.bfloat16)
    for e in range(experts):
        out_ref[e, 0] = contract(picks_ref[e], normed, 1, 0).astype(jnp.bfloat16)


def scaled_kernel(routes_ref, weight_ref, grad_ref, out_ref):
    experts, _, capacity, _ = out_ref.shape
    picks = selections(routes_ref[...], experts, capacity)
    weight = as_column(weight_ref[...])
    scaled = (weight * grad_ref[...].astype(jnp.float32)).astype(jnp.bfloat16)
    for e in range(experts):
        out_ref[e, 0] = contract(picks[e], scaled, 1, 0).astype(jnp.bfloat16)


def to_experts(kernel, arrays, specs, experts, capacity, quarter, scratch=()):
    sent = pl.pallas_call(
        kernel,
        out_shape=jax.ShapeDtypeStruct((experts, 4, capacity, quarter), jnp.bfloat16),
        grid=(4,),
        in_specs=specs,
        out_specs=pl.BlockSpec((experts, 1, capacity, quarter), lambda q: (0, q, 0, 0)),
        scratch_shapes=list(scratch),
        **kernel_settings(1 << 29, 1 << 23),
    )(*arrays)
    return sent.reshape(experts * 4, capacity, quarter)


def whole_block(array):
    return pl.BlockSpec(array.shape, lambda *_: (0,) * array.ndim)


def normed_to_experts(routes, tokens, norm, experts, capacity):
    tok_count, width = tokens.shape
    return to_experts(
        normed_kernel,
        (routes, tokens, norm),
        [whole_block(routes), whole_block(tokens), whole_block(norm)],
        experts,
        capacity,
        width // 4,
        [
            pltpu.VMEM((experts, capacity, tok_count), jnp.bfloat16),
            pltpu.VMEM((tok_count, 1), jnp.float32),
        ],
    )


def scaled_to_experts(routes, weight, grads, experts, capacity):
    tok_count, width = grads.shape
    return to_experts(
        scaled_kernel,
        (routes, weight, grads),
        [
            whole_block(routes),
            whole_block(weight),
            pl.BlockSpec((tok_count, width // 4), lambda q: (0, q)),
        ],
        experts,
        capacity,
        width // 4,
    )


def placed_back(picks, returned_ref, q):
    mixed = 0.0
    for e, pick in enumerate(picks):
        mixed = mixed + contract(pick, returned_ref[4 * e + q], 0, 0)
    return mixed


def forward_end_kernel(routes_ref, weight_ref, tokens_ref, returned_ref, out_ref):
    shard_count, capacity, quarter = returned_ref.shape
    picks = selections(routes_ref[...], shard_count // 4, capacity)
    weight = as_column(weight_ref[...])
    for q in range(4):
        columns = slice(q * quarter, (q + 1) * quarter)
        tokens = tokens_ref[:, columns].astype(jnp.float32)
        mixed = placed_back(picks, returned_ref, q)
        out_ref[:, columns] = (tokens + weight * mixed).astype(jnp.bfloat16)


def backward_first_kernel(routes_ref, tokens_ref, grad_ref, norm_ref, returned_ref, out_ref, factors_ref):
    shard_count, capacity, sent = returned_ref.shape
    width = sent - 128
    model_width = tokens_ref.shape[1]
    quarter = model_width // 4
    picks = selections(routes_ref[...], shard_count // 4, capacity)
    inv_rms = inverse_rms(tokens_ref, quarter)
    along = 0.0
    for q in range(4):
        for e, pick in enumerate(picks):
            along = along + contract(pick, returned_ref[4 * e + q, :, width:], 0, 0)
    along = 0.25 * jnp.sum(along, axis=1, keepdims=True)
    shrink = along * (1.0 / model_width) * inv_rms * inv_rms
    lane = lax.broadcasted_iota(jnp.int32, factors_ref.shape, 1)
    factors_ref[...] = jnp.where(lane == 0, inv_rms, shrink)
    for q in range(4):
        columns = slice(q * quarter, q * quarter + width)
        pulled = 0.0
        for e, pick in enumerate(picks):
            pulled = pulled + contract(pick, returned_ref[4 * e + q, :, :width], 0, 0)
        pulled = pulled * norm_ref[:, columns].astype(jnp.float32)
        values = tokens_ref[:, columns].astype(jnp.float32)
        own = grad_ref[:, columns].astype(jnp.float32)
        out_ref[:, q * width : (q + 1) * width] = (
            own + (pulled * inv_rms - values * shrink)
        ).astype(jnp.bfloat16)


def backward_second_kernel(routes_ref, tokens_ref, grad_ref, norm_ref, factors_ref, returned_ref, out_ref):
    shard_count, capacity, width = returned_ref.shape
    quarter = tokens_ref.shape[1] // 4
    picks = selections(routes_ref[...], shard_count // 4, capacity)
    inv_rms = factors_ref[:, 0:1]
    shrink = factors_ref[:, 1:2]
    for q in range(4):
        columns = slice((q + 1) * quarter - width, (q + 1) * quarter)
        pulled = placed_back(picks, returned_ref, q) * norm_ref[:, columns].astype(jnp.float32)
        values = tokens_ref[:, columns].astype(jnp.float32)
        own = grad_ref[:, columns].astype(jnp.float32)
        out_ref[:, q * width : (q + 1) * width] = (
            own + (pulled * inv_rms - values * shrink)
        ).astype(jnp.bfloat16)


def copy_kernel(piece_ref, out_ref):
    out_ref[...] = piece_ref[...]


def joined_kernel(first_ref, second_ref, out_ref):
    first = first_ref.shape[1] // 4
    second = second_ref.shape[1] // 4
    for q in range(4):
        begin = q * (first + second)
        out_ref[:, begin : begin + first] = first_ref[:, q * first : (q + 1) * first]
        out_ref[:, begin + first : begin + first + second] = second_ref[
            :, q * second : (q + 1) * second
        ]


def kernel_settings(flops, moved, vmem=VMEM_BYTES):
    return dict(
        compiler_params=pltpu.CompilerParams(vmem_limit_bytes=vmem),
        cost_estimate=pl.CostEstimate(flops=flops, bytes_accessed=moved, transcendentals=0),
    )


def local_call(kernel, shapes, *arrays, flops=1 << 28):
    whole = pl.BlockSpec(memory_space=pltpu.VMEM)
    return pl.pallas_call(
        kernel,
        out_shape=shapes,
        in_specs=[whole] * len(arrays),
        out_specs=jax.tree.map(lambda _: whole, shapes),
        **kernel_settings(flops, 1 << 22, LOCAL_VMEM_BYTES),
    )(*arrays)


def paired_product(rows, weight, weight_dim, core):
    product = contract(rows, weight, 1, weight_dim).astype(jnp.bfloat16)
    product = product.reshape(2, -1, product.shape[1])
    product = lax.optimization_barrier(product)
    own = lax.dynamic_index_in_dim(product, core, 0, keepdims=False)
    other = lax.dynamic_index_in_dim(product, 1 - core, 0, keepdims=False)
    came = from_partner(other, "ep", 0)
    return (own.astype(jnp.float32) + came.astype(jnp.float32)).astype(jnp.bfloat16)


def both_halves(own, core, earlier=()):
    other = after(from_partner(own, "ep", 0), earlier)
    first = jnp.where(core == 0, own, other)
    second = jnp.where(core == 0, other, own)
    return jnp.concatenate([first, second], axis=0)


def whole_sum(paired, distant):
    return paired.astype(jnp.float32) + distant.astype(jnp.float32)


def shards(
    section_input,
    forward_routes,
    forward_weight,
    saved_input,
    section_grad,
    backward_routes,
    backward_weight,
    norm_gain,
    w_gate,
    w_up,
    w_down,
):
    experts = lax.axis_size("ep") // 4
    tok_count, model_width = section_input.shape[1:]
    capacity = tok_count * 5 // (4 * experts)
    quarter = model_width // 4
    core = (lax.axis_index("ep") & 1)
    gate_w = w_gate[0, 0]
    up_w = w_up[0, 0]
    down_w = w_down[0, 0]
    hidden_width = gate_w.shape[1]
    shape = (4 * experts, capacity, quarter)
    whole = jax.ShapeDtypeStruct((tok_count, model_width), jnp.bfloat16)
    widths = (quarter * 3 // 7, quarter * 4 // 7)
    fwd_tokens = section_input[0]
    fwd_routes = forward_routes.reshape(1, tok_count)
    bwd_tokens = saved_input[0]
    cotangent = section_grad[0]
    bwd_routes = backward_routes.reshape(1, tok_count)

    send_fwd = normed_to_experts(fwd_routes, fwd_tokens, norm_gain, experts, capacity)
    send_rows = normed_to_experts(bwd_routes, bwd_tokens, norm_gain, experts, capacity)
    send_grads = scaled_to_experts(bwd_routes, backward_weight, cotangent, experts, capacity)

    got_fwd = exchange(send_fwd)
    got_rows = exchange(after(send_rows, got_fwd))

    fwd_rows = got_fwd.reshape(-1, quarter)
    bwd_rows = got_rows.reshape(-1, quarter)

    fwd_gate = paired_product(fwd_rows, gate_w, 0, core)
    fwd_gate_distant = from_partner(fwd_gate, "ep", 1)
    fwd_up = paired_product(fwd_rows, up_w, 0, core)
    fwd_up_distant = from_partner(fwd_up, "ep", 1)

    got_grads = exchange(after(send_grads, (got_rows, fwd_gate, fwd_up)))
    grad_rows = got_grads.reshape(-1, quarter)
    bwd_gate = paired_product(after(bwd_rows, fwd_gate_distant), gate_w, 0, core)
    bwd_gate_distant = from_partner(bwd_gate, "ep", 1)
    bwd_up = paired_product(after(bwd_rows, fwd_up_distant), up_w, 0, core)
    bwd_up_distant = from_partner(bwd_up, "ep", 1)

    gate_pre = whole_sum(fwd_gate, after(fwd_gate_distant, (bwd_gate, bwd_up)))
    up_pre = whole_sum(fwd_up, fwd_up_distant)
    hidden = both_halves(
        (gate_pre * jax.nn.sigmoid(gate_pre) * up_pre).astype(jnp.bfloat16), core
    )
    fwd_result = contract(hidden, down_w, 1, 0).astype(jnp.bfloat16)
    fwd_returned = exchange(after(fwd_result, got_grads).reshape(shape))

    hidden_grad = paired_product(after(grad_rows, bwd_gate_distant), down_w, 1, core)
    hidden_grad_distant = from_partner(after(hidden_grad, (bwd_up_distant, fwd_result)), "ep", 1)
    gate_pre = whole_sum(bwd_gate, bwd_gate_distant)
    up_pre = whole_sum(bwd_up, bwd_up_distant)
    hidden_grad = whole_sum(hidden_grad, hidden_grad_distant)
    sigmoid_gate = jax.nn.sigmoid(gate_pre)
    gate_grad = hidden_grad * up_pre * sigmoid_gate * (1.0 + gate_pre * (1.0 - sigmoid_gate))
    up_grad = hidden_grad * gate_pre * sigmoid_gate
    along = jnp.sum(gate_grad * gate_pre + up_grad * up_pre, axis=1, keepdims=True)
    high = lax.reduce_precision(along, 8, 7)
    lane = lax.broadcasted_iota(jnp.int32, (along.shape[0], 128), 1)
    along = jnp.where(lane == 0, high, jnp.where(lane == 1, along - high, 0.0))
    grads = jnp.concatenate([gate_grad, up_grad, along], axis=1).astype(jnp.bfloat16)
    grads = both_halves(grads, core, fwd_returned)
    gate_grad = grads[:, :hidden_width]
    up_grad = grads[:, hidden_width : 2 * hidden_width]
    along = grads[:, 2 * hidden_width :]

    def input_grads(begin, end):
        result = contract(gate_grad, gate_w[begin:end], 1, 1)
        return (result + contract(up_grad, up_w[begin:end], 1, 1)).astype(jnp.bfloat16)

    first = jnp.concatenate([input_grads(0, widths[0]), along], axis=1)
    first_back = exchange(first.reshape(4 * experts, capacity, -1))
    second = input_grads(widths[0], quarter)

    layer_out = local_call(
        forward_end_kernel, whole, fwd_routes, forward_weight, fwd_tokens, fwd_returned
    )
    arrived_input = passed_along(after(layer_out, first_back), "pp", 1)

    second = after(second, (first_back, layer_out))
    second_back = exchange(second.reshape(4 * experts, capacity, -1))
    first_out, factors = local_call(
        backward_first_kernel,
        [
            jax.ShapeDtypeStruct((tok_count, 4 * widths[0]), jnp.bfloat16),
            jax.ShapeDtypeStruct((tok_count, 128), jnp.float32),
        ],
        bwd_routes,
        bwd_tokens,
        cotangent,
        norm_gain,
        first_back,
    )
    second_out = local_call(
        backward_second_kernel,
        jax.ShapeDtypeStruct((tok_count, 4 * widths[1]), jnp.bfloat16),
        bwd_routes,
        bwd_tokens,
        cotangent,
        norm_gain,
        factors,
        second_back,
    )
    arrived_input = local_call(copy_kernel, whole, after(arrived_input, second_out))
    first_out = passed_along(first_out, "pp", -1)
    first_out = local_call(
        copy_kernel, jax.ShapeDtypeStruct(first_out.shape, jnp.bfloat16), first_out, flops=1 << 40
    )
    second_out = passed_along(second_out, "pp", -1)
    arrived_grad = local_call(joined_kernel, whole, first_out, second_out)
    return (arrived_input[None], arrived_grad[None])


def solution(mesh):
    specs = (
        P("pp", "ep", None),
        P("pp", "ep", None),
        P("pp", "ep"),
        P("pp", "ep", None),
        P("pp", "ep", None),
        P("pp", "ep", None),
        P("pp", "ep"),
        P("pp", None),
        P("pp", "ep", None, None),
        P("pp", "ep", None, None),
        P("pp", "ep", None, None),
    )
    return jax.shard_map(
        shards,
        mesh=mesh,
        in_specs=specs,
        out_specs=(P("pp", "ep", None), P("pp", "ep", None)),
        check_vma=False,
    )
```

```python
import functools

import jax
import jax.numpy as jnp
from jax import lax
from jax.experimental import pallas as pl
from jax.experimental.pallas import tpu as pltpu
from jax.sharding import PartitionSpec as P

epsilon = 1e-06
VMEM_BYTES = 60 * 1024 * 1024
LOCAL_VMEM_BYTES = 36 * 1024 * 1024


def from_partner(value, axis, bit):
    return lax.ppermute(value, axis, [(i, i ^ 1 << bit) for i in range(lax.axis_size(axis))])


def passed_along(value, axis, by):
    count = lax.axis_size(axis)
    return lax.ppermute(value, axis, [(i, (i + by) % count) for i in range(count)])


def exchange(value):
    return lax.all_to_all(value, "ep", split_axis=0, concat_axis=0, tiled=True)


def after(value, earlier):
    return lax.optimization_barrier((value, earlier))[0]


def contract(left, right, left_dim, right_dim):
    return lax.dot_general(
        left, right, (((left_dim,), (right_dim,)), ((), ())), preferred_element_type=jnp.float32
    )


def selections(routes, experts, capacity):
    tok_count = routes.shape[1]
    padded = 8 * pl.cdiv(experts, 8)
    named = routes == lax.broadcasted_iota(jnp.int32, (padded, tok_count), 0)
    earlier = lax.broadcasted_iota(jnp.int32, (tok_count, tok_count), 0) < lax.broadcasted_iota(
        jnp.int32, (tok_count, tok_count), 1
    )
    places = contract(
        named.astype(jnp.float32).astype(jnp.bfloat16),
        earlier.astype(jnp.float32).astype(jnp.bfloat16),
        1,
        0,
    )
    places = jnp.where(named, places, -1.0)
    slots = lax.broadcasted_iota(jnp.int32, (capacity, tok_count), 0).astype(jnp.float32)
    return [
        (places[e : e + 1, :] == slots).astype(jnp.float32).astype(jnp.bfloat16)
        for e in range(experts)
    ]


def as_column(row):
    count = row.shape[1]
    diagonal = lax.broadcasted_iota(jnp.int32, (count, count), 0) == lax.broadcasted_iota(
        jnp.int32, (count, count), 1
    )
    return jnp.sum(jnp.where(diagonal, row, 0.0), axis=1, keepdims=True)


def inverse_rms(tokens_ref, quarter):
    width = tokens_ref.shape[1]
    total = 0.0
    for q in range(width // quarter):
        values = tokens_ref[:, q * quarter : (q + 1) * quarter].astype(jnp.float32)
        total = total + jnp.sum(values * values, axis=1, keepdims=True)
    return lax.rsqrt(total * (1.0 / width) + epsilon)


def normed_kernel(routes_ref, tokens_ref, norm_ref, out_ref, picks_ref, inv_rms_ref):
    experts, _, capacity, quarter = out_ref.shape
    q = pl.program_id(0)

    @pl.when(q == 0)
    def _():
        for e, pick in enumerate(selections(routes_ref[...], experts, capacity)):
            picks_ref[e] = pick
        inv_rms_ref[...] = inverse_rms(tokens_ref, quarter)

    columns = pl.ds(pl.multiple_of(q * quarter, 128), quarter)
    values = tokens_ref[:, columns].astype(jnp.float32)
    norm = norm_ref[:, columns].astype(jnp.float32)
    normed = (values * inv_rms_ref[...] * norm).astype(jnp.bfloat16)
    for e in range(experts):
        out_ref[e, 0] = contract(picks_ref[e], normed, 1, 0).astype(jnp.bfloat16)


def scaled_kernel(routes_ref, weight_ref, grad_ref, out_ref):
    experts, _, capacity, _ = out_ref.shape
    picks = selections(routes_ref[...], experts, capacity)
    weight = as_column(weight_ref[...])
    scaled = (weight * grad_ref[...].astype(jnp.float32)).astype(jnp.bfloat16)
    for e in range(experts):
        out_ref[e, 0] = contract(picks[e], scaled, 1, 0).astype(jnp.bfloat16)


def to_experts(kernel, arrays, specs, experts, capacity, quarter, scratch=()):
    sent = pl.pallas_call(
        kernel,
        out_shape=jax.ShapeDtypeStruct((experts, 4, capacity, quarter), jnp.bfloat16),
        grid=(4,),
        in_specs=specs,
        out_specs=pl.BlockSpec((experts, 1, capacity, quarter), lambda q: (0, q, 0, 0)),
        scratch_shapes=list(scratch),
        **kernel_settings(1 << 29, 1 << 23),
    )(*arrays)
    return sent.reshape(experts * 4, capacity, quarter)


def whole_block(array):
    return pl.BlockSpec(array.shape, lambda *_: (0,) * array.ndim)


def normed_to_experts(routes, tokens, norm, experts, capacity):
    tok_count, width = tokens.shape
    return to_experts(
        normed_kernel,
        (routes, tokens, norm),
        [whole_block(routes), whole_block(tokens), whole_block(norm)],
        experts,
        capacity,
        width // 4,
        [
            pltpu.VMEM((experts, capacity, tok_count), jnp.bfloat16),
            pltpu.VMEM((tok_count, 1), jnp.float32),
        ],
    )


def scaled_to_experts(routes, weight, grads, experts, capacity):
    tok_count, width = grads.shape
    return to_experts(
        scaled_kernel,
        (routes, weight, grads),
        [
            whole_block(routes),
            whole_block(weight),
            pl.BlockSpec((tok_count, width // 4), lambda q: (0, q)),
        ],
        experts,
        capacity,
        width // 4,
    )


def placed_back(picks, returned_ref, q):
    mixed = 0.0
    for e, pick in enumerate(picks):
        mixed = mixed + contract(pick, returned_ref[4 * e + q], 0, 0)
    return mixed


def forward_end_kernel(routes_ref, weight_ref, tokens_ref, returned_ref, out_ref):
    shard_count, capacity, quarter = returned_ref.shape
    picks = selections(routes_ref[...], shard_count // 4, capacity)
    weight = as_column(weight_ref[...])
    for q in range(4):
        columns = slice(q * quarter, (q + 1) * quarter)
        tokens = tokens_ref[:, columns].astype(jnp.float32)
        mixed = placed_back(picks, returned_ref, q)
        out_ref[:, columns] = (tokens + weight * mixed).astype(jnp.bfloat16)


def backward_first_kernel(routes_ref, tokens_ref, grad_ref, norm_ref, returned_ref, out_ref, factors_ref):
    shard_count, capacity, sent = returned_ref.shape
    width = sent - 128
    model_width = tokens_ref.shape[1]
    quarter = model_width // 4
    picks = selections(routes_ref[...], shard_count // 4, capacity)
    inv_rms = inverse_rms(tokens_ref, quarter)
    along = 0.0
    for q in range(4):
        for e, pick in enumerate(picks):
            along = along + contract(pick, returned_ref[4 * e + q, :, width:], 0, 0)
    along = 0.25 * jnp.sum(along, axis=1, keepdims=True)
    shrink = along * (1.0 / model_width) * inv_rms * inv_rms
    lane = lax.broadcasted_iota(jnp.int32, factors_ref.shape, 1)
    factors_ref[...] = jnp.where(lane == 0, inv_rms, shrink)
    for q in range(4):
        columns = slice(q * quarter, q * quarter + width)
        pulled = 0.0
        for e, pick in enumerate(picks):
            pulled = pulled + contract(pick, returned_ref[4 * e + q, :, :width], 0, 0)
        pulled = pulled * norm_ref[:, columns].astype(jnp.float32)
        values = tokens_ref[:, columns].astype(jnp.float32)
        own = grad_ref[:, columns].astype(jnp.float32)
        out_ref[:, q * width : (q + 1) * width] = (
            own + (pulled * inv_rms - values * shrink)
        ).astype(jnp.bfloat16)


def backward_second_kernel(routes_ref, tokens_ref, grad_ref, norm_ref, factors_ref, returned_ref, out_ref):
    shard_count, capacity, width = returned_ref.shape
    quarter = tokens_ref.shape[1] // 4
    picks = selections(routes_ref[...], shard_count // 4, capacity)
    inv_rms = factors_ref[:, 0:1]
    shrink = factors_ref[:, 1:2]
    for q in range(4):
        columns = slice((q + 1) * quarter - width, (q + 1) * quarter)
        pulled = placed_back(picks, returned_ref, q) * norm_ref[:, columns].astype(jnp.float32)
        values = tokens_ref[:, columns].astype(jnp.float32)
        own = grad_ref[:, columns].astype(jnp.float32)
        out_ref[:, q * width : (q + 1) * width] = (
            own + (pulled * inv_rms - values * shrink)
        ).astype(jnp.bfloat16)


def copy_kernel(piece_ref, out_ref):
    out_ref[...] = piece_ref[...]


def joined_kernel(first_ref, second_ref, out_ref):
    first = first_ref.shape[1] // 4
    second = second_ref.shape[1] // 4
    for q in range(4):
        begin = q * (first + second)
        out_ref[:, begin : begin + first] = first_ref[:, q * first : (q + 1) * first]
        out_ref[:, begin + first : begin + first + second] = second_ref[
            :, q * second : (q + 1) * second
        ]


def kernel_settings(flops, moved, vmem=VMEM_BYTES):
    return dict(
        compiler_params=pltpu.CompilerParams(vmem_limit_bytes=vmem),
        cost_estimate=pl.CostEstimate(flops=flops, bytes_accessed=moved, transcendentals=0),
    )


def local_call(kernel, shapes, *arrays, flops=1 << 28):
    whole = pl.BlockSpec(memory_space=pltpu.VMEM)
    return pl.pallas_call(
        kernel,
        out_shape=shapes,
        in_specs=[whole] * len(arrays),
        out_specs=jax.tree.map(lambda _: whole, shapes),
        **kernel_settings(flops, 1 << 22, LOCAL_VMEM_BYTES),
    )(*arrays)


def paired_product(rows, weight, weight_dim, core):
    product = contract(rows, weight, 1, weight_dim).astype(jnp.bfloat16)
    product = product.reshape(2, -1, product.shape[1])
    product = lax.optimization_barrier(product)
    own = lax.dynamic_index_in_dim(product, core, 0, keepdims=False)
    other = lax.dynamic_index_in_dim(product, 1 - core, 0, keepdims=False)
    came = from_partner(other, "ep", 0)
    return (own.astype(jnp.float32) + came.astype(jnp.float32)).astype(jnp.bfloat16)


def both_halves(own, core, earlier=()):
    other = after(from_partner(own, "ep", 0), earlier)
    first = jnp.where(core == 0, own, other)
    second = jnp.where(core == 0, other, own)
    return jnp.concatenate([first, second], axis=0)


def whole_sum(paired, distant):
    return paired.astype(jnp.float32) + distant.astype(jnp.float32)


def shards(
    section_input,
    forward_routes,
    forward_weight,
    saved_input,
    section_grad,
    backward_routes,
    backward_weight,
    norm_gain,
    w_gate,
    w_up,
    w_down,
):
    experts = lax.axis_size("ep") // 4
    tok_count, model_width = section_input.shape[1:]
    capacity = tok_count * 5 // (4 * experts)
    quarter = model_width // 4
    core = (lax.axis_index("ep") & 1)
    gate_w = w_gate[0, 0]
    up_w = w_up[0, 0]
    down_w = w_down[0, 0]
    hidden_width = gate_w.shape[1]
    shape = (4 * experts, capacity, quarter)
    whole = jax.ShapeDtypeStruct((tok_count, model_width), jnp.bfloat16)
    widths = (quarter * 3 // 7, quarter * 4 // 7)
    fwd_tokens = section_input[0]
    fwd_routes = forward_routes.reshape(1, tok_count)
    bwd_tokens = saved_input[0]
    cotangent = section_grad[0]
    bwd_routes = backward_routes.reshape(1, tok_count)

    send_fwd = normed_to_experts(fwd_routes, fwd_tokens, norm_gain, experts, capacity)
    send_rows = normed_to_experts(bwd_routes, bwd_tokens, norm_gain, experts, capacity)
    send_grads = scaled_to_experts(bwd_routes, backward_weight, cotangent, experts, capacity)

    got_fwd = exchange(send_fwd)
    got_rows = exchange(after(send_rows, got_fwd))

    fwd_rows = got_fwd.reshape(-1, quarter)
    bwd_rows = got_rows.reshape(-1, quarter)

    fwd_gate = paired_product(fwd_rows, gate_w, 0, core)
    fwd_gate_distant = from_partner(fwd_gate, "ep", 1)
    fwd_up = paired_product(fwd_rows, up_w, 0, core)
    fwd_up_distant = from_partner(fwd_up, "ep", 1)

    got_grads = exchange(after(send_grads, (got_rows, fwd_gate, fwd_up)))
    grad_rows = got_grads.reshape(-1, quarter)
    bwd_gate = paired_product(after(bwd_rows, fwd_gate_distant), gate_w, 0, core)
    bwd_gate_distant = from_partner(bwd_gate, "ep", 1)
    bwd_up = paired_product(after(bwd_rows, fwd_up_distant), up_w, 0, core)
    bwd_up_distant = from_partner(bwd_up, "ep", 1)

    gate_pre = whole_sum(fwd_gate, after(fwd_gate_distant, (bwd_gate, bwd_up)))
    up_pre = whole_sum(fwd_up, fwd_up_distant)
    hidden = both_halves(
        (gate_pre * jax.nn.sigmoid(gate_pre) * up_pre).astype(jnp.bfloat16), core
    )
    fwd_result = contract(hidden, down_w, 1, 0).astype(jnp.bfloat16)
    fwd_returned = exchange(after(fwd_result, got_grads).reshape(shape))

    hidden_grad = paired_product(after(grad_rows, bwd_gate_distant), down_w, 1, core)
    hidden_grad_distant = from_partner(after(hidden_grad, (bwd_up_distant, fwd_result)), "ep", 1)
    gate_pre = whole_sum(bwd_gate, bwd_gate_distant)
    up_pre = whole_sum(bwd_up, bwd_up_distant)
    hidden_grad = whole_sum(hidden_grad, hidden_grad_distant)
    sigmoid_gate = jax.nn.sigmoid(gate_pre)
    gate_grad = hidden_grad * up_pre * sigmoid_gate * (1.0 + gate_pre * (1.0 - sigmoid_gate))
    up_grad = hidden_grad * gate_pre * sigmoid_gate
    along = jnp.sum(gate_grad * gate_pre + up_grad * up_pre, axis=1, keepdims=True)
    high = lax.reduce_precision(along, 8, 7)
    lane = lax.broadcasted_iota(jnp.int32, (along.shape[0], 128), 1)
    along = jnp.where(lane == 0, high, jnp.where(lane == 1, along - high, 0.0))
    grads = jnp.concatenate([gate_grad, up_grad, along], axis=1).astype(jnp.bfloat16)
    grads = both_halves(grads, core, fwd_returned)
    gate_grad = grads[:, :hidden_width]
    up_grad = grads[:, hidden_width : 2 * hidden_width]
    along = grads[:, 2 * hidden_width :]

    def input_grads(begin, end):
        result = contract(gate_grad, gate_w[begin:end], 1, 1)
        return (result + contract(up_grad, up_w[begin:end], 1, 1)).astype(jnp.bfloat16)

    first = jnp.concatenate([input_grads(0, widths[0]), along], axis=1)
    first_back = exchange(first.reshape(4 * experts, capacity, -1))
    second = input_grads(widths[0], quarter)

    layer_out = local_call(
        forward_end_kernel, whole, fwd_routes, forward_weight, fwd_tokens, fwd_returned
    )
    arrived_input = passed_along(after(layer_out, first_back), "pp", 1)

    second = after(second, (first_back, layer_out))
    second_back = exchange(second.reshape(4 * experts, capacity, -1))
    first_out, factors = local_call(
        backward_first_kernel,
        [
            jax.ShapeDtypeStruct((tok_count, 4 * widths[0]), jnp.bfloat16),
            jax.ShapeDtypeStruct((tok_count, 128), jnp.float32),
        ],
        bwd_routes,
        bwd_tokens,
        cotangent,
        norm_gain,
        first_back,
    )
    second_out = local_call(
        backward_second_kernel,
        jax.ShapeDtypeStruct((tok_count, 4 * widths[1]), jnp.bfloat16),
        bwd_routes,
        bwd_tokens,
        cotangent,
        norm_gain,
        factors,
        second_back,
    )
    first_out = passed_along(first_out, "pp", -1)
    first_out = local_call(
        copy_kernel, jax.ShapeDtypeStruct(first_out.shape, jnp.bfloat16), first_out, flops=1 << 40
    )
    second_out = passed_along(second_out, "pp", -1)
    arrived_grad = local_call(joined_kernel, whole, first_out, second_out)
    arrived_input = local_call(copy_kernel, whole, after(arrived_input, arrived_grad))
    return (arrived_input[None], arrived_grad[None])


def solution(mesh):
    specs = (
        P("pp", "ep", None),
        P("pp", "ep", None),
        P("pp", "ep"),
        P("pp", "ep", None),
        P("pp", "ep", None),
        P("pp", "ep", None),
        P("pp", "ep"),
        P("pp", None),
        P("pp", "ep", None, None),
        P("pp", "ep", None, None),
        P("pp", "ep", None, None),
    )
    return jax.shard_map(
        shards,
        mesh=mesh,
        in_specs=specs,
        out_specs=(P("pp", "ep", None), P("pp", "ep", None)),
        check_vma=False,
    )
```

```python
import functools

import jax
import jax.numpy as jnp
from jax import lax
from jax.experimental import pallas as pl
from jax.experimental.pallas import tpu as pltpu
from jax.sharding import PartitionSpec as P

epsilon = 1e-06
VMEM_BYTES = 60 * 1024 * 1024
LOCAL_VMEM_BYTES = 36 * 1024 * 1024


def from_partner(value, axis, bit):
    return lax.ppermute(value, axis, [(i, i ^ 1 << bit) for i in range(lax.axis_size(axis))])


def passed_along(value, axis, by):
    count = lax.axis_size(axis)
    return lax.ppermute(value, axis, [(i, (i + by) % count) for i in range(count)])


def exchange(value):
    return lax.all_to_all(value, "ep", split_axis=0, concat_axis=0, tiled=True)


def after(value, earlier):
    return lax.optimization_barrier((value, earlier))[0]


def contract(left, right, left_dim, right_dim):
    return lax.dot_general(
        left, right, (((left_dim,), (right_dim,)), ((), ())), preferred_element_type=jnp.float32
    )


def selections(routes, experts, capacity):
    tok_count = routes.shape[1]
    padded = 8 * pl.cdiv(experts, 8)
    named = routes == lax.broadcasted_iota(jnp.int32, (padded, tok_count), 0)
    earlier = lax.broadcasted_iota(jnp.int32, (tok_count, tok_count), 0) < lax.broadcasted_iota(
        jnp.int32, (tok_count, tok_count), 1
    )
    places = contract(
        named.astype(jnp.float32).astype(jnp.bfloat16),
        earlier.astype(jnp.float32).astype(jnp.bfloat16),
        1,
        0,
    )
    places = jnp.where(named, places, -1.0)
    slots = lax.broadcasted_iota(jnp.int32, (capacity, tok_count), 0).astype(jnp.float32)
    return [
        (places[e : e + 1, :] == slots).astype(jnp.float32).astype(jnp.bfloat16)
        for e in range(experts)
    ]


def as_column(row):
    count = row.shape[1]
    diagonal = lax.broadcasted_iota(jnp.int32, (count, count), 0) == lax.broadcasted_iota(
        jnp.int32, (count, count), 1
    )
    return jnp.sum(jnp.where(diagonal, row, 0.0), axis=1, keepdims=True)


def inverse_rms(tokens_ref, quarter):
    width = tokens_ref.shape[1]
    total = 0.0
    for q in range(width // quarter):
        values = tokens_ref[:, q * quarter : (q + 1) * quarter].astype(jnp.float32)
        total = total + jnp.sum(values * values, axis=1, keepdims=True)
    return lax.rsqrt(total * (1.0 / width) + epsilon)


def normed_kernel(routes_ref, *refs):
    parts, (norm_ref, out_ref, picks_ref, inv_rms_ref) = refs[:4], refs[4:]
    experts, _, capacity, quarter = out_ref.shape
    q = pl.program_id(0)

    @pl.when(q == 0)
    def _():
        for e, pick in enumerate(selections(routes_ref[...], experts, capacity)):
            picks_ref[e] = pick
        total = 0.0
        for part in parts:
            values = part[...].astype(jnp.float32)
            total = total + jnp.sum(values * values, axis=1, keepdims=True)
        inv_rms_ref[...] = lax.rsqrt(total * (1.0 / (4 * quarter)) + epsilon)

    for k, part in enumerate(parts):

        @pl.when(q == k)
        def _(k=k, part=part):
            norm = norm_ref[:, k * quarter : (k + 1) * quarter].astype(jnp.float32)
            values = part[...].astype(jnp.float32)
            normed = (values * inv_rms_ref[...] * norm).astype(jnp.bfloat16)
            for e in range(experts):
                out_ref[e, 0] = contract(picks_ref[e], normed, 1, 0).astype(jnp.bfloat16)


def scaled_kernel(routes_ref, weight_ref, grad_ref, out_ref):
    experts, _, capacity, _ = out_ref.shape
    picks = selections(routes_ref[...], experts, capacity)
    weight = as_column(weight_ref[...])
    scaled = (weight * grad_ref[...].astype(jnp.float32)).astype(jnp.bfloat16)
    for e in range(experts):
        out_ref[e, 0] = contract(picks[e], scaled, 1, 0).astype(jnp.bfloat16)


def to_experts(kernel, arrays, specs, experts, capacity, quarter, scratch=()):
    sent = pl.pallas_call(
        kernel,
        out_shape=jax.ShapeDtypeStruct((experts, 4, capacity, quarter), jnp.bfloat16),
        grid=(4,),
        in_specs=specs,
        out_specs=pl.BlockSpec((experts, 1, capacity, quarter), lambda q: (0, q, 0, 0)),
        scratch_shapes=list(scratch),
        **kernel_settings(1 << 29, 1 << 23),
    )(*arrays)
    return sent.reshape(experts * 4, capacity, quarter)


def whole_block(array):
    return pl.BlockSpec(array.shape, lambda *_: (0,) * array.ndim)


def normed_to_experts(routes, tokens, norm, experts, capacity):
    tok_count, width = tokens.shape
    return to_experts(
        normed_kernel,
        (routes, *[tokens] * 4, norm),
        [
            whole_block(routes),
            *[pl.BlockSpec((tok_count, width // 4), lambda q, k=k: (0, k)) for k in range(4)],
            whole_block(norm),
        ],
        experts,
        capacity,
        width // 4,
        [
            pltpu.VMEM((experts, capacity, tok_count), jnp.bfloat16),
            pltpu.VMEM((tok_count, 1), jnp.float32),
        ],
    )


def scaled_to_experts(routes, weight, grads, experts, capacity):
    tok_count, width = grads.shape
    return to_experts(
        scaled_kernel,
        (routes, weight, grads),
        [
            whole_block(routes),
            whole_block(weight),
            pl.BlockSpec((tok_count, width // 4), lambda q: (0, q)),
        ],
        experts,
        capacity,
        width // 4,
    )


def placed_back(picks, returned_ref, q):
    mixed = 0.0
    for e, pick in enumerate(picks):
        mixed = mixed + contract(pick, returned_ref[4 * e + q], 0, 0)
    return mixed


def forward_end_kernel(routes_ref, weight_ref, tokens_ref, returned_ref, out_ref):
    shard_count, capacity, quarter = returned_ref.shape
    picks = selections(routes_ref[...], shard_count // 4, capacity)
    weight = as_column(weight_ref[...])
    for q in range(4):
        columns = slice(q * quarter, (q + 1) * quarter)
        tokens = tokens_ref[:, columns].astype(jnp.float32)
        mixed = placed_back(picks, returned_ref, q)
        out_ref[:, columns] = (tokens + weight * mixed).astype(jnp.bfloat16)


def backward_first_kernel(routes_ref, tokens_ref, grad_ref, norm_ref, returned_ref, out_ref, factors_ref):
    shard_count, capacity, sent = returned_ref.shape
    width = sent - 128
    model_width = tokens_ref.shape[1]
    quarter = model_width // 4
    picks = selections(routes_ref[...], shard_count // 4, capacity)
    inv_rms = inverse_rms(tokens_ref, quarter)
    along = 0.0
    for q in range(4):
        for e, pick in enumerate(picks):
            along = along + contract(pick, returned_ref[4 * e + q, :, width:], 0, 0)
    along = 0.25 * jnp.sum(along, axis=1, keepdims=True)
    shrink = along * (1.0 / model_width) * inv_rms * inv_rms
    lane = lax.broadcasted_iota(jnp.int32, factors_ref.shape, 1)
    factors_ref[...] = jnp.where(lane == 0, inv_rms, shrink)
    for q in range(4):
        columns = slice(q * quarter, q * quarter + width)
        pulled = 0.0
        for e, pick in enumerate(picks):
            pulled = pulled + contract(pick, returned_ref[4 * e + q, :, :width], 0, 0)
        pulled = pulled * norm_ref[:, columns].astype(jnp.float32)
        values = tokens_ref[:, columns].astype(jnp.float32)
        own = grad_ref[:, columns].astype(jnp.float32)
        out_ref[:, q * width : (q + 1) * width] = (
            own + (pulled * inv_rms - values * shrink)
        ).astype(jnp.bfloat16)


def backward_second_kernel(routes_ref, tokens_ref, grad_ref, norm_ref, factors_ref, returned_ref, out_ref):
    shard_count, capacity, width = returned_ref.shape
    quarter = tokens_ref.shape[1] // 4
    picks = selections(routes_ref[...], shard_count // 4, capacity)
    inv_rms = factors_ref[:, 0:1]
    shrink = factors_ref[:, 1:2]
    for q in range(4):
        columns = slice((q + 1) * quarter - width, (q + 1) * quarter)
        pulled = placed_back(picks, returned_ref, q) * norm_ref[:, columns].astype(jnp.float32)
        values = tokens_ref[:, columns].astype(jnp.float32)
        own = grad_ref[:, columns].astype(jnp.float32)
        out_ref[:, q * width : (q + 1) * width] = (
            own + (pulled * inv_rms - values * shrink)
        ).astype(jnp.bfloat16)


def copy_kernel(piece_ref, out_ref):
    out_ref[...] = piece_ref[...]


def joined_kernel(first_ref, second_ref, out_ref):
    first = first_ref.shape[1] // 4
    second = second_ref.shape[1] // 4
    for q in range(4):
        begin = q * (first + second)
        out_ref[:, begin : begin + first] = first_ref[:, q * first : (q + 1) * first]
        out_ref[:, begin + first : begin + first + second] = second_ref[
            :, q * second : (q + 1) * second
        ]


def kernel_settings(flops, moved, vmem=VMEM_BYTES):
    return dict(
        compiler_params=pltpu.CompilerParams(vmem_limit_bytes=vmem),
        cost_estimate=pl.CostEstimate(flops=flops, bytes_accessed=moved, transcendentals=0),
    )


def local_call(kernel, shapes, *arrays, flops=1 << 28):
    whole = pl.BlockSpec(memory_space=pltpu.VMEM)
    return pl.pallas_call(
        kernel,
        out_shape=shapes,
        in_specs=[whole] * len(arrays),
        out_specs=jax.tree.map(lambda _: whole, shapes),
        **kernel_settings(flops, 1 << 22, LOCAL_VMEM_BYTES),
    )(*arrays)


def paired_product(rows, weight, weight_dim, core):
    product = contract(rows, weight, 1, weight_dim).astype(jnp.bfloat16)
    product = product.reshape(2, -1, product.shape[1])
    product = lax.optimization_barrier(product)
    own = lax.dynamic_index_in_dim(product, core, 0, keepdims=False)
    other = lax.dynamic_index_in_dim(product, 1 - core, 0, keepdims=False)
    came = from_partner(other, "ep", 0)
    return (own.astype(jnp.float32) + came.astype(jnp.float32)).astype(jnp.bfloat16)


def both_halves(own, core, earlier=()):
    other = after(from_partner(own, "ep", 0), earlier)
    first = jnp.where(core == 0, own, other)
    second = jnp.where(core == 0, other, own)
    return jnp.concatenate([first, second], axis=0)


def whole_sum(paired, distant):
    return paired.astype(jnp.float32) + distant.astype(jnp.float32)


def shards(
    section_input,
    forward_routes,
    forward_weight,
    saved_input,
    section_grad,
    backward_routes,
    backward_weight,
    norm_gain,
    w_gate,
    w_up,
    w_down,
):
    experts = lax.axis_size("ep") // 4
    tok_count, model_width = section_input.shape[1:]
    capacity = tok_count * 5 // (4 * experts)
    quarter = model_width // 4
    core = (lax.axis_index("ep") & 1)
    gate_w = w_gate[0, 0]
    up_w = w_up[0, 0]
    down_w = w_down[0, 0]
    hidden_width = gate_w.shape[1]
    shape = (4 * experts, capacity, quarter)
    whole = jax.ShapeDtypeStruct((tok_count, model_width), jnp.bfloat16)
    widths = (quarter * 3 // 7, quarter * 4 // 7)
    fwd_tokens = section_input[0]
    fwd_routes = forward_routes.reshape(1, tok_count)
    bwd_tokens = saved_input[0]
    cotangent = section_grad[0]
    bwd_routes = backward_routes.reshape(1, tok_count)

    send_fwd = normed_to_experts(fwd_routes, fwd_tokens, norm_gain, experts, capacity)
    send_rows = normed_to_experts(bwd_routes, bwd_tokens, norm_gain, experts, capacity)
    send_grads = scaled_to_experts(bwd_routes, backward_weight, cotangent, experts, capacity)

    got_fwd = exchange(send_fwd)
    got_rows = exchange(after(send_rows, got_fwd))

    fwd_rows = got_fwd.reshape(-1, quarter)
    bwd_rows = got_rows.reshape(-1, quarter)

    fwd_gate = paired_product(fwd_rows, gate_w, 0, core)
    fwd_gate_distant = from_partner(fwd_gate, "ep", 1)
    fwd_up = paired_product(fwd_rows, up_w, 0, core)
    fwd_up_distant = from_partner(fwd_up, "ep", 1)

    got_grads = exchange(after(send_grads, (got_rows, fwd_gate, fwd_up)))
    grad_rows = got_grads.reshape(-1, quarter)
    bwd_gate = paired_product(after(bwd_rows, fwd_gate_distant), gate_w, 0, core)
    bwd_gate_distant = from_partner(bwd_gate, "ep", 1)
    bwd_up = paired_product(after(bwd_rows, fwd_up_distant), up_w, 0, core)
    bwd_up_distant = from_partner(bwd_up, "ep", 1)

    gate_pre = whole_sum(fwd_gate, after(fwd_gate_distant, (bwd_gate, bwd_up)))
    up_pre = whole_sum(fwd_up, fwd_up_distant)
    hidden = both_halves(
        (gate_pre * jax.nn.sigmoid(gate_pre) * up_pre).astype(jnp.bfloat16), core
    )
    fwd_result = contract(hidden, down_w, 1, 0).astype(jnp.bfloat16)
    fwd_returned = exchange(after(fwd_result, got_grads).reshape(shape))

    hidden_grad = paired_product(after(grad_rows, bwd_gate_distant), down_w, 1, core)
    hidden_grad_distant = from_partner(after(hidden_grad, (bwd_up_distant, fwd_result)), "ep", 1)
    gate_pre = whole_sum(bwd_gate, bwd_gate_distant)
    up_pre = whole_sum(bwd_up, bwd_up_distant)
    hidden_grad = whole_sum(hidden_grad, hidden_grad_distant)
    sigmoid_gate = jax.nn.sigmoid(gate_pre)
    gate_grad = hidden_grad * up_pre * sigmoid_gate * (1.0 + gate_pre * (1.0 - sigmoid_gate))
    up_grad = hidden_grad * gate_pre * sigmoid_gate
    along = jnp.sum(gate_grad * gate_pre + up_grad * up_pre, axis=1, keepdims=True)
    high = lax.reduce_precision(along, 8, 7)
    lane = lax.broadcasted_iota(jnp.int32, (along.shape[0], 128), 1)
    along = jnp.where(lane == 0, high, jnp.where(lane == 1, along - high, 0.0))
    grads = jnp.concatenate([gate_grad, up_grad, along], axis=1).astype(jnp.bfloat16)
    grads = both_halves(grads, core, fwd_returned)
    gate_grad = grads[:, :hidden_width]
    up_grad = grads[:, hidden_width : 2 * hidden_width]
    along = grads[:, 2 * hidden_width :]

    def input_grads(begin, end):
        result = contract(gate_grad, gate_w[begin:end], 1, 1)
        return (result + contract(up_grad, up_w[begin:end], 1, 1)).astype(jnp.bfloat16)

    first = jnp.concatenate([input_grads(0, widths[0]), along], axis=1)
    first_back = exchange(first.reshape(4 * experts, capacity, -1))
    second = input_grads(widths[0], quarter)

    layer_out = local_call(
        forward_end_kernel, whole, fwd_routes, forward_weight, fwd_tokens, fwd_returned
    )
    arrived_input = passed_along(after(layer_out, first_back), "pp", 1)

    second = after(second, (first_back, layer_out))
    second_back = exchange(second.reshape(4 * experts, capacity, -1))
    first_out, factors = local_call(
        backward_first_kernel,
        [
            jax.ShapeDtypeStruct((tok_count, 4 * widths[0]), jnp.bfloat16),
            jax.ShapeDtypeStruct((tok_count, 128), jnp.float32),
        ],
        bwd_routes,
        bwd_tokens,
        cotangent,
        norm_gain,
        first_back,
    )
    second_out = local_call(
        backward_second_kernel,
        jax.ShapeDtypeStruct((tok_count, 4 * widths[1]), jnp.bfloat16),
        bwd_routes,
        bwd_tokens,
        cotangent,
        norm_gain,
        factors,
        second_back,
    )
    first_out = passed_along(first_out, "pp", -1)
    first_out = local_call(
        copy_kernel, jax.ShapeDtypeStruct(first_out.shape, jnp.bfloat16), first_out, flops=1 << 40
    )
    second_out = passed_along(second_out, "pp", -1)
    arrived_grad = local_call(joined_kernel, whole, first_out, second_out)
    arrived_input = local_call(copy_kernel, whole, after(arrived_input, arrived_grad))
    return (arrived_input[None], arrived_grad[None])


def solution(mesh):
    specs = (
        P("pp", "ep", None),
        P("pp", "ep", None),
        P("pp", "ep"),
        P("pp", "ep", None),
        P("pp", "ep", None),
        P("pp", "ep", None),
        P("pp", "ep"),
        P("pp", None),
        P("pp", "ep", None, None),
        P("pp", "ep", None, None),
        P("pp", "ep", None, None),
    )
    return jax.shard_map(
        shards,
        mesh=mesh,
        in_specs=specs,
        out_specs=(P("pp", "ep", None), P("pp", "ep", None)),
        check_vma=False,
    )
```
